1024 devices in a mesh: dp: 16 (over x, core), expert: 64 (over y, z).
Axes of the slice: x: 8, y: 8, z: 8, core: 2. Of those that a mesh axis runs over, the one named last changes fastest.
Arguments:
- tokens: bfloat16 [12288, 3584], P('expert'), may hold values from -6 to 6
- routes: int32 [12288, 2], P('expert'), may hold values from 0 to 63, all different within a row
- gates: float32 [12288, 2], P('expert'), may hold values from 0.1 to 0.9
- clusters: int32 [12288, 2], P('expert'), may hold values from 0 to 15
- counts: int32 [64, 64], P('expert'), may hold values from 1 to 2
- w_in: bfloat16 [64, 3584, 2432], P('expert', None, 'dp'), may hold values from -0.09375 to 0.09375
- w_out: bfloat16 [64, 2432, 3584], P('expert', 'dp'), may hold values from -0.125 to 0.125
- cotangent: bfloat16 [12288, 3584], P('expert'), may hold values from -6 to 6
Outputs:
- mixed: bfloat16 [12288, 3584], P('expert', 'dp')
- grad_tokens: bfloat16 [12288, 3584], P('expert', 'dp')
- grad_w_in: bfloat16 [64, 3584, 2432], P('expert', None, 'dp')
The draws below stay inside these ranges and needn't reach their ends.
Inputs may be any that keep to these rules, and one draw needn't show every extreme that they name: `routes`: each token names two different experts, and every expert is named by some token.
All inputs are finite; a program needn't handle non-finite values.
Results may differ from the reference program's by a relative error of at most 0.0064.
Values may be sent and summed in bfloat16 or wider, within the bound.
A program may use at most 32 MiB of HBM per device.

```python
import jax
import jax.numpy as jnp
from jax import lax

D = 3584
FF = 2432
TOK_DEV = 192
SLOTS = 2
EXPERTS = 64
TOKENS = 12288
N_DP = 16
N_EXPERT = 64


def touch_ends(drawn, own_key, low, high):
    longest = drawn.shape.index(max(drawn.shape))
    spots = []
    for shift in (0, 1):
        where = [jax.random.randint(jax.random.fold_in(own_key, axis), (), 0, length) for axis, length in enumerate(drawn.shape)]
        where[longest] = (where[longest] + shift) % drawn.shape[longest]
        spots.append(tuple(where))
    return drawn.at[spots[0]].set(low).at[spots[1]].set(high)


def shard_levels(key, dims, split, low, top_value):
    factor_of, own = 1.0, jax.random.fold_in(key, 6)
    for position, shards_of in split:
        steps = jnp.exp(jax.random.uniform(jax.random.fold_in(own, position), (shards_of,), jnp.float32, low / len(split), top_value / len(split)))
        factor_of = factor_of * jnp.repeat(steps, dims[position] // shards_of).reshape([-1 if axis == position else 1 for axis in range(len(dims))])
    return factor_of


def different_ones(own_key, rows, number_of, top, lift):
    order = jax.random.permutation(jax.random.fold_in(own_key, 1), number_of)
    favour = order
    for power in range(3):
        favour = favour * favour // number_of
    favour = favour * lift // number_of
    tickets = jax.random.randint(jax.random.fold_in(own_key, 2), (rows, number_of), 0, 4096) + favour
    fixed_rows = jax.random.permutation(jax.random.fold_in(own_key, 3), rows)[jnp.arange(number_of) % rows]
    tickets = jnp.where(jnp.arange(rows)[:, None] == fixed_rows[None, :], 1 << 14, tickets)
    merit = tickets * number_of + jnp.arange(number_of)
    return lax.top_k(merit.astype(jnp.int32), top)[1].astype(jnp.int32)


def noise(own_key, extent, spread, most, pieces=(), held_as=jnp.bfloat16):
    entries = spread * jax.random.normal(own_key, extent, jnp.float32)
    if pieces:
        entries = entries * shard_levels(own_key, extent, pieces, -0.22, 0.18)
    return jnp.clip(entries, -most, most).astype(held_as)


def setup_inputs(seed: int = 0) -> dict:
    seeds = jax.random.split(jax.random.key(seed), 9)
    tokens = noise(seeds[0], (TOKENS, D), 1.0, 6.0, ((0, 64),))
    routes = different_ones(seeds[1], TOKENS, EXPERTS, 2, 256)
    gates = jnp.clip(0.1 + 0.79999997 * jax.random.uniform(seeds[2], (TOKENS, 2), jnp.float32) ** shard_levels(seeds[2], (TOKENS, 2), ((0, 64),), -0.2, 0.2), 0.1, 0.9)
    clusters = touch_ends(jax.random.randint(seeds[3], (TOKENS, 2), 0, 16), jax.random.fold_in(seeds[3], 1), 0, 15).astype(jnp.int32)
    counts = touch_ends(jax.random.randint(seeds[4], (N_EXPERT, EXPERTS), 1, SLOTS + 1), jax.random.fold_in(seeds[4], 1), 1, SLOTS).astype(jnp.int32)
    w_in = noise(seeds[5], (EXPERTS, D, FF), D ** -0.5, 0.09375, ((0, 64), (2, 16)))
    w_out = noise(seeds[6], (EXPERTS, FF, D), FF ** -0.5, 0.125, ((0, 64), (1, 16)))
    cotangent = noise(seeds[7], (TOKENS, D), 1.0, 6.0, ((0, 64),))
    return {"tokens": tokens, "routes": routes, "gates": gates, "clusters": clusters, "counts": counts, "w_in": w_in, "w_out": w_out, "cotangent": cotangent}


precise = lax.Precision.HIGHEST


def pool_block(tokens, routes, gates, clusters, counts, cotangent):
    slot_width = EXPERTS * SLOTS
    live_count = jnp.take(counts, routes)
    slot_ids = routes * SLOTS + jnp.remainder(clusters, live_count)
    slot_lanes = jnp.arange(slot_width, dtype=jnp.int32)
    picked = (slot_ids[:, :, None] == slot_lanes[None, None, :]).astype(jnp.float32)
    either = jnp.sum(picked, axis=1)
    weighted = jnp.sum(picked * gates[:, :, None], axis=1)
    member = jnp.maximum(jnp.sum(either, axis=0), 1.0)
    pooled_sum = jnp.dot(either.T, tokens.astype(jnp.float32), precision=precise)
    centroids = (pooled_sum / member[:, None]).astype(jnp.bfloat16)
    back_pooled = jnp.dot(weighted.T, cotangent.astype(jnp.float32), precision=precise)
    return centroids, back_pooled, either, weighted, member


def blocked_sum(left, right, form):
    partial_terms = jnp.einsum(form, left.astype(jnp.float32), right.astype(jnp.float32), precision=precise)
    rounded = lax.optimization_barrier(partial_terms.astype(jnp.bfloat16))
    return jnp.sum(rounded.astype(jnp.float32), axis=0)


def expert_pass(operands):
    centre_rows, back_rows, weight_in, weight_out = operands
    row_total = centre_rows.shape[0]
    unit_count = FF // N_DP
    preact = jnp.dot(centre_rows, weight_in, preferred_element_type=jnp.float32)
    hidden_grad = lax.dot_general(back_rows, weight_out, (((1,), (1,)), ((), ())), preferred_element_type=jnp.float32)
    hidden = jax.nn.silu(preact).astype(jnp.bfloat16)
    sigmoid_val = jax.nn.sigmoid(preact)
    preact_grad = (hidden_grad * sigmoid_val * (1.0 + preact * (1.0 - sigmoid_val))).astype(jnp.bfloat16)
    expert_out = blocked_sum(hidden.reshape(row_total, N_DP, unit_count), weight_out.reshape(N_DP, unit_count, D),
                             "rpf,pfd->prd").astype(jnp.bfloat16)
    centre_grad = blocked_sum(preact_grad.reshape(row_total, N_DP, unit_count), weight_in.reshape(D, N_DP, unit_count),
                              "rpf,dpf->prd").astype(jnp.bfloat16)
    weight_grad = jnp.dot(centre_rows.T, preact_grad, preferred_element_type=jnp.float32).astype(jnp.bfloat16)
    return expert_out, centre_grad, weight_grad


def decode_block(tokens, gates, cotangent, centroids, back_pooled, either, weighted, member, expert_out, centre_grad):
    gate_sum = 1.0 + jnp.sum(gates, axis=1)
    carried = expert_out.astype(jnp.float32) - centroids.astype(jnp.float32)
    mixed = tokens.astype(jnp.float32) * gate_sum[:, None] + jnp.dot(weighted, carried, precision=precise)
    pulled = (centre_grad.astype(jnp.float32) - back_pooled) / member[:, None]
    grad_tokens = cotangent.astype(jnp.float32) * gate_sum[:, None] + jnp.dot(either, pulled, precision=precise)
    return mixed.astype(jnp.bfloat16), grad_tokens.astype(jnp.bfloat16)


def split_blocks(array):
    return array.reshape((N_EXPERT, TOK_DEV) + array.shape[1:])


def to_experts(per_source):
    return per_source.reshape(N_EXPERT, EXPERTS, SLOTS, D).transpose(1, 0, 2, 3).reshape(EXPERTS, N_EXPERT * SLOTS, D)


def to_sources(per_expert):
    return per_expert.reshape(EXPERTS, N_EXPERT, SLOTS, D).transpose(1, 0, 2, 3).reshape(N_EXPERT, EXPERTS * SLOTS, D)


def reference(tokens, routes, gates, clusters, counts, w_in, w_out, cotangent):
    centroids, back_pooled, either, weighted, member = jax.vmap(pool_block)(
        split_blocks(tokens), split_blocks(routes), split_blocks(gates), split_blocks(clusters), counts, split_blocks(cotangent))
    expert_out, centre_grad, weight_grad = lax.map(
        expert_pass, (to_experts(centroids), to_experts(back_pooled.astype(jnp.bfloat16)), w_in, w_out))
    mixed, grad_tokens = jax.vmap(decode_block)(
        split_blocks(tokens), split_blocks(gates), split_blocks(cotangent), centroids, back_pooled, either, weighted, member,
        to_sources(expert_out), to_sources(centre_grad))
    return mixed.reshape(TOKENS, D), grad_tokens.reshape(TOKENS, D), weight_grad
```

```python
import functools

import jax
import jax.numpy as jnp
from jax import lax
from jax.experimental import pallas as pl
from jax.experimental.pallas import tpu as pltpu
from jax.sharding import PartitionSpec as P

SLOTS = 2
LANES = 128
CHIPS = 8
MESH = pl.DeviceIdType.MESH
BF16 = jnp.bfloat16
F32 = jnp.float32
REACH = (4, 3, 5, 2, 6, 1, 7, 0)


def nn(a, b):
    return lax.dot_general(a, b, (((1,), (0,)), ((), ())), preferred_element_type=F32)


def nt(a, b):
    return lax.dot_general(a, b, (((1,), (1,)), ((), ())), preferred_element_type=F32)


def split(value):
    high = value.astype(BF16)
    return high, (value - high.astype(F32)).astype(BF16)


def eye(size):
    rows = lax.broadcasted_iota(jnp.int32, (size, size), 0)
    return (rows == lax.broadcasted_iota(jnp.int32, (size, size), 1)).astype(BF16)


def kernel(
    shape,
    tokens, routes, gates, clusters, counts, w_in, w_out, cotangent,
    mixed_out, grad_tokens_out, grad_w_out,
    tok_win, cot_win, routes_v, gates_v, clusters_v, counts_v, win_v, wout_v,
    win_t, wout_t, wout_q, perm, perm_t,
    either_t, weight_t, either_r, weight_r, gate_col, member_v, tok_s, cot_s, centre_v, back_v,
    send1, recv1, send2, recv2,
    gathered, pre_v, part, sib_out, sib_in, right_out, left_out, right_in, left_in, far_out, far_in,
    mixed_v, grad_v, gw_v,
    in_sem, hop_sem, ag_send, ag_recv, rs_send, rs_recv, out_sem,
):
    experts, toks, feats, units = shape
    slots = experts * SLOTS
    half = feats // 2
    upper = feats - LANES
    dp = lax.axis_index("dp")
    me = lax.axis_index("expert")
    chip = dp // 2
    core = lax.rem(dp, 2)
    right = lax.rem(chip + 1, CHIPS) * 2 + core
    left = lax.rem(chip + CHIPS - 1, CHIPS) * 2 + core
    sibling = chip * 2 + 1 - core

    def shard(distance, of_core):
        return lax.rem(chip + distance, CHIPS) * 2 + of_core

    width = tokens.shape[1]
    window = tok_win.shape[1]
    tile = jnp.minimum(dp * feats // LANES, (width - window) // LANES)
    start = pl.multiple_of(tile * LANES, LANES)
    shift = dp * feats - tile * LANES

    loads = [
        pltpu.make_async_copy(src, dst, in_sem.at[i])
        for i, (src, dst) in enumerate((
            (routes, routes_v), (clusters, clusters_v), (gates, gates_v), (counts, counts_v),
            (tokens.at[:, pl.ds(start, window)], tok_win),
            (cotangent.at[:, pl.ds(start, window)], cot_win),
            (w_out.at[0], wout_v), (w_in.at[0], win_v),
        ))
    ]
    for load in loads:
        load.start()

    barrier = pltpu.get_barrier_semaphore()

    @pl.loop(1, experts)
    def _(k):
        pl.semaphore_signal(
            barrier, inc=1, device_id=(dp, lax.rem(me + k, experts)), device_id_type=MESH
        )

    for there in (right, left, sibling):
        pl.semaphore_signal(barrier, inc=1, device_id=(there, me), device_id_type=MESH)

    rows = lax.broadcasted_iota(jnp.int32, (4 * slots, 4 * slots), 0)
    cols = lax.broadcasted_iota(jnp.int32, (4 * slots, 4 * slots), 1)
    perm[...] = (cols == ((rows % 8) // 2) * slots + (rows // 8) * 2 + rows % 2).astype(F32).astype(BF16)
    perm_t[...] = (rows == ((cols % 8) // 2) * slots + (cols // 8) * 2 + cols % 2).astype(F32).astype(BF16)

    for load in loads[:4]:
        load.wait()
    expert_rows = lax.broadcasted_iota(jnp.int32, (experts, experts), 0)
    expert_cols = lax.broadcasted_iota(jnp.int32, (experts, experts), 1)
    live_col = jnp.sum(jnp.where(expert_rows == expert_cols, counts_v[...], 0), axis=1, keepdims=True)
    ids = lax.broadcasted_iota(jnp.int32, (experts, toks), 0)
    slot_rows = lax.broadcasted_iota(jnp.int32, (slots, toks), 0)
    hits, weights = [], []
    for k in range(2):
        route = routes_v[k : k + 1, :]
        live = jnp.sum(jnp.where(ids == route, live_col, 0), axis=0, keepdims=True)
        slot = route * SLOTS + jnp.where(live == 2, clusters_v[k : k + 1, :] & 1, 0)
        hits.append((slot_rows == slot).astype(F32))
        weights.append(hits[-1] * gates_v[k : k + 1, :])
    either = hits[0] + hits[1]
    weight_hi, weight_lo = split(weights[0] + weights[1])
    member = jnp.maximum(jnp.sum(either, axis=1, keepdims=True), 1.0)
    member_v[...] = jnp.broadcast_to(member, member_v.shape)
    either_t[...] = either.astype(BF16)
    weight_t[0] = weight_hi
    weight_t[1] = weight_lo

    pick_rows = lax.broadcasted_iota(jnp.int32, (window, 2 * LANES), 0)
    pick_cols = lax.broadcasted_iota(jnp.int32, (window, 2 * LANES), 1)
    pick = ((pick_rows == pick_cols + shift) & (pick_cols < feats)).astype(F32).astype(BF16)
    loads[4].wait()
    tok_s[...] = nn(tok_win[...], pick).astype(BF16)
    centre_v[...] = (nn(either_t[...], tok_s[...]) / member_v[...]).astype(BF16)
    loads[5].wait()
    cot_s[...] = nn(cot_win[...], pick).astype(BF16)
    back = nn(weight_t[0], cot_s[...]) + nn(weight_t[1], cot_s[...])
    back_v[...] = back
    sent = back.astype(BF16)
    stacked = jnp.concatenate(
        [centre_v[:, :LANES], centre_v[:, LANES:], sent[:, :LANES], sent[:, LANES:]], axis=0
    )
    send1[...] = nn(perm[...], stacked).astype(BF16).reshape(experts, 8, LANES)

    def exchange(send, recv, sem):
        own = pltpu.make_async_copy(send.at[me], recv.at[me], hop_sem.at[sem])
        own.start()

        @pl.loop(1, experts)
        def _(k):
            peer = lax.rem(me + k, experts)
            pltpu.make_async_remote_copy(
                src_ref=send.at[peer], dst_ref=recv.at[me],
                send_sem=hop_sem.at[sem + 1], recv_sem=hop_sem.at[sem + 2],
                device_id=(dp, peer), device_id_type=MESH,
            ).start()

        return own

    def exchanged(own, send, recv, sem):
        own.wait()
        rest = pl.ds(0, experts - 1)
        pltpu.make_async_copy(recv.at[rest], recv.at[rest], hop_sem.at[sem + 2]).wait()

    def sent_all(send, sem):
        rest = pl.ds(0, experts - 1)
        pltpu.make_async_copy(send.at[rest], send.at[rest], hop_sem.at[sem + 1]).wait()

    pl.semaphore_wait(barrier, experts + 2)
    own1 = exchange(send1, recv1, 0)

    token_eye = eye(toks)
    either_r[...] = nt(token_eye, either_t[...]).astype(BF16)
    weight_r[0] = nt(token_eye, weight_t[0]).astype(BF16)
    weight_r[1] = nt(token_eye, weight_t[1]).astype(BF16)
    gate_row = 1.0 + jnp.sum(gates_v[...], axis=0, keepdims=True)
    gate_col[...] = jnp.broadcast_to(
        jnp.sum(jnp.where(token_eye.astype(F32) > 0.0, gate_row, 0.0), axis=1, keepdims=True), gate_col.shape
    )
    loads[6].wait()
    lane_eye = eye(LANES)

    @pl.loop(0, width // LANES)
    def _(j):
        at = pl.multiple_of(j * LANES, LANES)
        wout_t[pl.ds(at, LANES), :] = nt(lane_eye, wout_v[:, pl.ds(at, LANES)]).astype(BF16)

    loads[7].wait()
    unit_eye = eye(units)

    @pl.loop(0, 2 * CHIPS)
    def _(q):
        at = pl.ds(pl.multiple_of(q * feats, 32), feats)
        win_t[q] = nt(unit_eye, win_v[at, :]).astype(BF16)
        wout_q[q] = nt(unit_eye, wout_t[at, :]).astype(BF16)

    exchanged(own1, send1, recv1, 0)
    arrived = lax.dot_general(
        recv1[...].reshape(4 * slots, LANES), perm[...], (((0,), (0,)), ((), ())), preferred_element_type=F32
    ).astype(BF16)
    for kind in range(2):
        gathered[kind, dp, 0:LANES, :] = arrived[:, 2 * kind * slots : (2 * kind + 1) * slots]
        gathered[kind, dp, LANES:feats, :] = arrived[0:upper, (2 * kind + 1) * slots : (2 * kind + 2) * slots]

    pending = []

    def pass_on(kind, lane, which, rows, there):
        at = pl.ds(*rows)
        copy = pltpu.make_async_remote_copy(
            src_ref=gathered.at[kind, which, at], dst_ref=gathered.at[kind, which, at],
            send_sem=ag_send.at[kind, lane], recv_sem=ag_recv.at[kind, lane],
            device_id=(there, me), device_id_type=MESH,
        )
        copy.start()
        pending.append(copy)

    def landed(kind, lane, which, rows):
        at = pl.ds(*rows)
        pltpu.make_async_copy(gathered.at[kind, which, at], gathered.at[kind, which, at], ag_recv.at[kind, lane]).wait()

    whole, first, second = (0, feats), (0, half), (half, half)
    for kind in range(2):
        pass_on(kind, 0, dp, whole, right)
        pass_on(kind, 4, dp, whole, left)
        pass_on(kind, 8, dp, whole, sibling)

    forms = (win_t, wout_q)

    def contract(kind, which):
        pre_v[kind] += nn(forms[kind][which], gathered[kind, which])

    for kind in range(2):
        pre_v[kind] = nn(forms[kind][dp], gathered[kind, dp])

    def step(kind, hop):
        behind, ahead = shard(CHIPS - hop, core), shard(hop, core)
        from_left = first if hop == 4 else whole
        from_right = second if hop == 4 else whole
        landed(kind, hop - 1, behind, from_left)
        if hop < 4:
            pass_on(kind, hop, behind, first if hop == 3 else whole, right)
        pass_on(kind, 8 + hop, behind, from_left, sibling)
        landed(kind, 3 + hop, ahead, from_right)
        if hop < 4:
            pass_on(kind, 4 + hop, ahead, second if hop == 3 else whole, left)
        pass_on(kind, 12 + hop, ahead, from_right, sibling)

    def use(kind, hop):
        if hop == 0:
            landed(kind, 8, sibling, whole)
            contract(kind, sibling)
            return
        contract(kind, shard(CHIPS - hop, core))
        if hop < 4:
            contract(kind, shard(hop, core))
        other = 1 - core
        landed(kind, 8 + hop, shard(CHIPS - hop, other), first if hop == 4 else whole)
        landed(kind, 12 + hop, shard(hop, other), second if hop == 4 else whole)
        contract(kind, shard(CHIPS - hop, other))
        if hop < 4:
            contract(kind, shard(hop, other))

    for hop in range(1, 5):
        for kind in range(2):
            step(kind, hop)
        for kind in range(2):
            use(kind, hop - 1)
    for kind in range(2):
        use(kind, 4)

    preact = pre_v[0]
    sigmoid_val = jax.nn.sigmoid(preact)
    hidden = (preact * sigmoid_val).astype(BF16)
    preact_grad = (pre_v[1] * sigmoid_val * (1.0 + preact * (1.0 - sigmoid_val))).astype(BF16)

    summed = []
    for kind, (weights_of, units_of) in enumerate(((wout_t, hidden), (win_v, preact_grad))):
        for d in REACH:
            theirs = pl.ds(pl.multiple_of(shard(d, 1 - core) * feats, 32), feats)
            sib_out[kind, d] = nn(weights_of[theirs, :], units_of).astype(BF16)
            copy = pltpu.make_async_remote_copy(
                src_ref=sib_out.at[kind, d], dst_ref=sib_in.at[kind, d],
                send_sem=rs_send.at[kind, d], recv_sem=rs_recv.at[kind, d],
                device_id=(sibling, me), device_id_type=MESH,
            )
            copy.start()
            summed.append(copy)
            ours = pl.ds(pl.multiple_of(shard(d, core) * feats, 32), feats)
            part[kind, d] = nn(weights_of[ours, :], units_of)

    def both(kind, d):
        pltpu.make_async_copy(sib_in.at[kind, d], sib_in.at[kind, d], rs_recv.at[kind, d]).wait()
        return part[kind, d] + sib_in[kind, d].astype(F32)

    def push(kind, lane, out, into, there):
        copy = pltpu.make_async_remote_copy(
            src_ref=out, dst_ref=into,
            send_sem=rs_send.at[kind, lane], recv_sem=rs_recv.at[kind, lane],
            device_id=(there, me), device_id_type=MESH,
        )
        copy.start()
        summed.append(copy)

    def came(kind, lane, into):
        pltpu.make_async_copy(into, into, rs_recv.at[kind, lane]).wait()
        return into[...].astype(F32)

    def chain(kind, hop):
        if hop == 0:
            total = both(kind, 4)
            far_out[kind, 0] = total[:half].astype(BF16)
            far_out[kind, 1] = total[half:].astype(BF16)
            push(kind, 8, far_out.at[kind, 0], far_in.at[kind, 0], right)
            push(kind, 12, far_out.at[kind, 1], far_in.at[kind, 1], left)
            return
        to_right, to_left = both(kind, 4 - hop), both(kind, 4 + hop)
        if hop == 1:
            right_out[kind, 0, :half] = (to_right[:half] + came(kind, 8, far_in.at[kind, 0])).astype(BF16)
            right_out[kind, 0, half:] = to_right[half:].astype(BF16)
            left_out[kind, 0, :half] = to_left[:half].astype(BF16)
            left_out[kind, 0, half:] = (to_left[half:] + came(kind, 12, far_in.at[kind, 1])).astype(BF16)
        else:
            right_out[kind, hop - 1] = (to_right + came(kind, 7 + hop, right_in.at[kind, hop - 2])).astype(BF16)
            left_out[kind, hop - 1] = (to_left + came(kind, 11 + hop, left_in.at[kind, hop - 2])).astype(BF16)
        push(kind, 8 + hop, right_out.at[kind, hop - 1], right_in.at[kind, hop - 1], right)
        push(kind, 12 + hop, left_out.at[kind, hop - 1], left_in.at[kind, hop - 1], left)

    def weight_grads(low, high):
        @pl.loop(low, high)
        def _(q):
            at = pl.ds(pl.multiple_of(q * feats, 32), feats)
            gw_v[at, :] = nt(gathered[0, q], preact_grad).astype(BF16)

    for hop in range(4):
        for kind in range(2):
            chain(kind, hop)
        weight_grads(4 * hop, 4 * hop + 4)
    gw_copy = pltpu.make_async_copy(gw_v, grad_w_out.at[0], out_sem.at[0])
    gw_copy.start()

    pieces = []
    for kind in range(2):
        total = both(kind, 0)
        total += came(kind, 11, right_in.at[kind, 2]) + came(kind, 15, left_in.at[kind, 2])
        total = total.astype(BF16)
        pieces += [total[:LANES], jnp.concatenate([total[LANES:], jnp.zeros((LANES - upper, slots), BF16)], axis=0)]
    send2[...] = nt(perm[...], jnp.concatenate(pieces, axis=1)).astype(BF16).reshape(experts, 8, LANES)
    own2 = exchange(send2, recv2, 3)

    scaled_tok = [tok_s[:, i * LANES : (i + 1) * LANES].astype(F32) * gate_col[...] for i in range(2)]
    scaled_cot = [cot_s[:, i * LANES : (i + 1) * LANES].astype(F32) * gate_col[...] for i in range(2)]
    scale = 1.0 / member_v[:, :LANES]
    for copy in pending + summed:
        copy.wait_send()
    sent_all(send1, 0)

    exchanged(own2, send2, recv2, 3)
    ordered = nn(perm_t[...], recv2[...].reshape(4 * slots, LANES))
    for i, (low, count) in enumerate(((0, LANES), (LANES, upper))):
        carried = ordered[i * slots : (i + 1) * slots] - centre_v[:, i * LANES : (i + 1) * LANES].astype(F32)
        pulled = (ordered[(2 + i) * slots : (3 + i) * slots] - back_v[:, i * LANES : (i + 1) * LANES]) * scale
        high, rest = split(carried)
        mixed = scaled_tok[i] + nn(weight_r[0], high) + nn(weight_r[0], rest) + nn(weight_r[1], high)
        mixed_v[:, low : low + count] = mixed[:, :count].astype(BF16)
        high, rest = split(pulled)
        grads = scaled_cot[i] + nn(either_r[...], high) + nn(either_r[...], rest)
        grad_v[:, low : low + count] = grads[:, :count].astype(BF16)
    mixed_copy = pltpu.make_async_copy(mixed_v, mixed_out, out_sem.at[1])
    mixed_copy.start()
    grad_copy = pltpu.make_async_copy(grad_v, grad_tokens_out, out_sem.at[2])
    grad_copy.start()
    sent_all(send2, 3)
    gw_copy.wait()
    mixed_copy.wait()
    grad_copy.wait()


def on_device(tokens, routes, gates, clusters, counts, w_in, w_out, cotangent):
    toks, width = tokens.shape
    experts = counts.shape[1]
    shards = lax.axis_size("dp")
    units = w_in.shape[2]
    feats = width // shards
    slots = experts * SLOTS
    vmem = pltpu.VMEM
    dma = pltpu.SemaphoreType.DMA
    scratch = [
        vmem((toks, 3 * LANES), BF16), vmem((toks, 3 * LANES), BF16),
        vmem((2, toks), jnp.int32), vmem((2, toks), F32), vmem((2, toks), jnp.int32), vmem((1, experts), jnp.int32),
        vmem((width, units), BF16), vmem((units, width), BF16),
        vmem((shards, units, feats), BF16), vmem((width, units), BF16), vmem((shards, units, feats), BF16),
        vmem((4 * slots, 4 * slots), BF16), vmem((4 * slots, 4 * slots), BF16),
        vmem((slots, toks), BF16), vmem((2, slots, toks), BF16),
        vmem((toks, slots), BF16), vmem((2, toks, slots), BF16),
        vmem((toks, LANES), F32), vmem((slots, 2 * LANES), F32),
        vmem((toks, 2 * LANES), BF16), vmem((toks, 2 * LANES), BF16),
        vmem((slots, 2 * LANES), BF16), vmem((slots, 2 * LANES), F32),
        vmem((experts, 8, LANES), BF16), vmem((experts, 8, LANES), BF16),
        vmem((experts, 8, LANES), BF16), vmem((experts, 8, LANES), BF16),
        vmem((2, shards, feats, slots), BF16), vmem((2, units, slots), F32),
        vmem((2, CHIPS, feats, slots), F32), vmem((2, CHIPS, feats, slots), BF16), vmem((2, CHIPS, feats, slots), BF16),
        vmem((2, 3, feats, slots), BF16), vmem((2, 3, feats, slots), BF16),
        vmem((2, 3, feats, slots), BF16), vmem((2, 3, feats, slots), BF16),
        vmem((2, 2, feats // 2, slots), BF16), vmem((2, 2, feats // 2, slots), BF16),
        vmem((toks, feats), BF16), vmem((toks, feats), BF16), vmem((width, units), BF16),
        dma((8,)), dma((6,)), dma((2, 17)), dma((2, 17)), dma((2, 16)), dma((2, 16)), dma((3,)),
    ]
    return pl.pallas_call(
        functools.partial(kernel, (experts, toks, feats, units)),
        out_shape=(
            jax.ShapeDtypeStruct((toks, feats), BF16),
            jax.ShapeDtypeStruct((toks, feats), BF16),
            jax.ShapeDtypeStruct((1, width, units), BF16),
        ),
        in_specs=[pl.BlockSpec(memory_space=pl.ANY)] * 8,
        out_specs=(pl.BlockSpec(memory_space=pl.ANY),) * 3,
        scratch_shapes=scratch,
        compiler_params=pltpu.CompilerParams(
            collective_id=0, has_side_effects=True, vmem_limit_bytes=48 * 1024 * 1024
        ),
    )(tokens, routes.T, gates.T, clusters.T, counts, w_in, w_out, cotangent)


def solution(mesh):
    in_specs = (
        P("expert", None),
        P("expert", None),
        P("expert", None),
        P("expert", None),
        P("expert", None),
        P("expert", None, "dp"),
        P("expert", "dp", None),
        P("expert", None),
    )
    out_specs = (P("expert", "dp"), P("expert", "dp"), P("expert", None, "dp"))
    return jax.shard_map(
        on_device, mesh=mesh, in_specs=in_specs, out_specs=out_specs, check_vma=False
    )
```

```python
import functools

import jax
import jax.numpy as jnp
from jax import lax
from jax.experimental import pallas as pl
from jax.experimental.pallas import tpu as pltpu
from jax.sharding import PartitionSpec as P

SLOTS = 2
LANES = 128
CHIPS = 8
MESH = pl.DeviceIdType.MESH
BF16 = jnp.bfloat16
F32 = jnp.float32

def nn(a, b):
    return lax.dot_general(a, b, (((1,), (0,)), ((), ())), preferred_element_type=F32)


def nt(a, b):
    return lax.dot_general(a, b, (((1,), (1,)), ((), ())), preferred_element_type=F32)


def split(value):
    high = value.astype(BF16)
    return high, (value - high.astype(F32)).astype(BF16)


def eye(size):
    rows = lax.broadcasted_iota(jnp.int32, (size, size), 0)
    return (rows == lax.broadcasted_iota(jnp.int32, (size, size), 1)).astype(BF16)


def kernel(
    shape,
    tokens, routes, gates, clusters, counts, w_in, w_out, cotangent,
    mixed_out, grad_tokens_out, grad_w_out,
    tok_win, cot_win, routes_v, gates_v, clusters_v, counts_v, win_v, wout_v,
    tok_q, cot_q, win_r, wout_r, perm, perm_t,
    either_t, weight_t, either_r, weight_r, gate_col, member_v, tok_s, cot_s, centre_v, back_v,
    send1, recv1, send2, recv2,
    gathered, pre_v, part, sib_out, sib_in, right_out, left_out, right_in, left_in,
    in_sem, hop_sem, ag_send, ag_recv, rs_send, rs_recv,
):
    experts, toks, feats, units = shape
    slots = experts * SLOTS
    half = feats // 2
    halves = ((0, half), (half, half))
    upper = feats - LANES
    dp = lax.axis_index("dp")
    me = lax.axis_index("expert")
    chip = dp // 2
    core = lax.rem(dp, 2)
    right = lax.rem(chip + 1, CHIPS) * 2 + core
    left = lax.rem(chip + CHIPS - 1, CHIPS) * 2 + core
    right_2 = lax.rem(chip + 2, CHIPS) * 2 + core
    left_2 = lax.rem(chip + CHIPS - 2, CHIPS) * 2 + core
    sibling = chip * 2 + 1 - core

    def far_first(i):
        if experts != CHIPS * CHIPS:
            return lax.rem(me + i + 1, experts)

        def away(j):
            return 4 + (j + 1) // 2 * (1 - 2 * (j % 2))

        row = lax.rem(me // CHIPS + away(i // CHIPS), CHIPS)
        column = lax.rem(lax.rem(me, CHIPS) + away(i % CHIPS), CHIPS)
        return row * CHIPS + column

    def shard(distance, of_core):
        return lax.rem(chip + distance, CHIPS) * 2 + of_core

    width = tokens.shape[1]
    window = tok_win.shape[1]
    tile = jnp.minimum(dp * feats // LANES, (width - window) // LANES)
    start = pl.multiple_of(tile * LANES, LANES)
    shift = dp * feats - tile * LANES
    quarter = width // 4
    parity = lax.rem(chip, 2)
    mine, near = 2 * parity + core, 2 * (1 - parity) + core
    own_quarter = pl.ds(pl.multiple_of(mine * quarter, LANES), quarter)

    loads = [
        pltpu.make_async_copy(src, dst, in_sem.at[i])
        for i, (src, dst) in enumerate((
            (routes, routes_v), (clusters, clusters_v), (gates, gates_v), (counts, counts_v),
            (tokens.at[:, own_quarter], tok_q),
            (cotangent.at[:, own_quarter], cot_q),
            (tokens.at[:, pl.ds(start, window)], tok_win),
            (cotangent.at[:, pl.ds(start, window)], cot_win),
            (w_out.at[0], wout_v), (w_in.at[0], win_v),
        ))
    ]
    for load in loads[:6]:
        load.start()

    barrier = pltpu.get_barrier_semaphore()

    @pl.loop(0, experts - 1)
    def _(i):
        pl.semaphore_signal(barrier, inc=1, device_id=(dp, far_first(i)), device_id_type=MESH)

    for there in (right, left, right_2, left_2, sibling):
        pl.semaphore_signal(barrier, inc=1, device_id=(there, me), device_id_type=MESH)

    for load in loads[6:]:
        load.start()

    rows = lax.broadcasted_iota(jnp.int32, (4 * slots, 4 * slots), 0)
    cols = lax.broadcasted_iota(jnp.int32, (4 * slots, 4 * slots), 1)
    perm[...] = (cols == ((rows % 8) // 2) * slots + (rows // 8) * 2 + rows % 2).astype(F32).astype(BF16)

    for load in loads[:4]:
        load.wait()
    expert_rows = lax.broadcasted_iota(jnp.int32, (experts, experts), 0)
    expert_cols = lax.broadcasted_iota(jnp.int32, (experts, experts), 1)
    live_col = jnp.sum(jnp.where(expert_rows == expert_cols, counts_v[...], 0), axis=1, keepdims=True)
    ids = lax.broadcasted_iota(jnp.int32, (experts, toks), 0)
    slot_rows = lax.broadcasted_iota(jnp.int32, (slots, toks), 0)
    hits, weights = [], []
    for k in range(2):
        route = routes_v[k : k + 1, :]
        live = jnp.sum(jnp.where(ids == route, live_col, 0), axis=0, keepdims=True)
        slot = route * SLOTS + jnp.where(live == 2, clusters_v[k : k + 1, :] & 1, 0)
        hits.append((slot_rows == slot).astype(F32))
        weights.append(hits[-1] * gates_v[k : k + 1, :])
    either = hits[0] + hits[1]
    weight_hi, weight_lo = split(weights[0] + weights[1])
    member = jnp.maximum(jnp.sum(either, axis=1, keepdims=True), 1.0)
    member_v[...] = jnp.broadcast_to(member, member_v.shape)
    either_t[...] = either.astype(BF16)
    weight_t[0] = weight_hi
    weight_t[1] = weight_lo

    def exchange(send, recv, sem):
        own = pltpu.make_async_copy(send.at[me], recv.at[me], hop_sem.at[sem])
        own.start()

        @pl.loop(0, experts - 1)
        def _(i):
            peer = far_first(i)
            pltpu.make_async_remote_copy(
                src_ref=send.at[peer], dst_ref=recv.at[me],
                send_sem=hop_sem.at[sem + 1], recv_sem=hop_sem.at[sem + 2],
                device_id=(dp, peer), device_id_type=MESH,
            ).start()

        return own

    def exchanged(own, send, recv, sem):
        own.wait()
        rest = pl.ds(0, experts - 1)
        pltpu.make_async_copy(recv.at[rest], recv.at[rest], hop_sem.at[sem + 2]).wait()

    def sent_all(send, sem):
        rest = pl.ds(0, experts - 1)
        pltpu.make_async_copy(send.at[rest], send.at[rest], hop_sem.at[sem + 1]).wait()

    def spread(rows_of):
        last = jnp.concatenate([rows_of[:, 6 * LANES :], jnp.zeros((slots, LANES), BF16)], axis=1)
        stacked = jnp.concatenate([rows_of[:, 2 * i * LANES : 2 * (i + 1) * LANES] for i in range(3)] + [last], axis=0)
        return nn(perm[...], stacked).astype(BF16).reshape(experts, 8, 2 * LANES)

    loads[4].wait()
    send1[0] = spread((nn(either_t[...], tok_q[...]) / member).astype(BF16))
    pl.semaphore_wait(barrier, experts + 4)
    owns = [exchange(send1.at[0], recv1.at[0], 0)]
    loads[5].wait()
    send1[1] = spread((nn(weight_t[0], cot_q[...]) + nn(weight_t[1], cot_q[...])).astype(BF16))
    owns.append(exchange(send1.at[1], recv1.at[1], 3))

    pick_rows = lax.broadcasted_iota(jnp.int32, (window, 2 * LANES), 0)
    pick_cols = lax.broadcasted_iota(jnp.int32, (window, 2 * LANES), 1)
    pick = ((pick_rows == pick_cols + shift) & (pick_cols < feats)).astype(F32).astype(BF16)
    loads[6].wait()
    tok_s[...] = nn(tok_win[...], pick).astype(BF16)
    centre_v[...] = (nn(either_t[...], tok_s[...]) / member_v[...]).astype(BF16)
    loads[7].wait()
    cot_s[...] = nn(cot_win[...], pick).astype(BF16)
    back_v[...] = nn(weight_t[0], cot_s[...]) + nn(weight_t[1], cot_s[...])
    perm_t[...] = (rows == ((cols % 8) // 2) * slots + (cols // 8) * 2 + cols % 2).astype(F32).astype(BF16)
    token_eye = eye(toks)
    either_r[...] = nt(token_eye, either_t[...]).astype(BF16)
    weight_r[0] = nt(token_eye, weight_t[0]).astype(BF16)
    weight_r[1] = nt(token_eye, weight_t[1]).astype(BF16)
    gate_row = 1.0 + jnp.sum(gates_v[...], axis=0, keepdims=True)
    gate_col[...] = jnp.broadcast_to(
        jnp.sum(jnp.where(token_eye.astype(F32) > 0.0, gate_row, 0.0), axis=1, keepdims=True), gate_col.shape
    )
    loads[8].wait()
    loads[9].wait()
    lane_eye = eye(2 * LANES)

    @pl.loop(0, width // (2 * LANES))
    def _(j):
        at = pl.ds(pl.multiple_of(j * 2 * LANES, LANES), 2 * LANES)
        win_r[at, :] = nt(lane_eye, win_v[:, at]).astype(BF16)
        wout_r[at, :] = nt(lane_eye, wout_v[:, at]).astype(BF16)

    pending = []

    def pass_on(kind, lane, which, rows, there):
        at = pl.ds(*rows)
        copy = pltpu.make_async_remote_copy(
            src_ref=gathered.at[kind, which, at], dst_ref=gathered.at[kind, which, at],
            send_sem=ag_send.at[kind, lane], recv_sem=ag_recv.at[kind, lane],
            device_id=(there, me), device_id_type=MESH,
        )
        copy.start()
        pending.append(copy)

    def landed(kind, lane, which, rows):
        here = gathered.at[kind, which, pl.ds(*rows)]
        pltpu.make_async_copy(here, here, ag_recv.at[kind, lane]).wait()

    whole, first, second = (0, quarter), (0, quarter // 2), (quarter // 2, quarter // 2)
    projections = (win_v, wout_v)

    def contract(kind, which):
        columns = pl.ds(pl.multiple_of(which * quarter, LANES), quarter)
        return nn(projections[kind][:, columns], gathered[kind, which])

    def arrive(kind):
        exchanged(owns[kind], send1.at[kind], recv1.at[kind], 3 * kind)
        arrived = lax.dot_general(
            recv1[kind].reshape(4 * slots, 2 * LANES), perm[...], (((0,), (0,)), ((), ())), preferred_element_type=F32
        ).astype(BF16)
        for i in range(4):
            count = 2 * LANES if i < 3 else LANES
            low = 2 * i * LANES
            gathered[kind, mine, low : low + count, :] = arrived[:count, i * slots : (i + 1) * slots]
        pass_on(kind, 0, mine, first, right)
        pass_on(kind, 1, mine, second, left)
        pass_on(kind, 2, mine, whole, sibling)
        pre_v[kind] = contract(kind, mine)

    def relay(kind):
        landed(kind, 0, near, first)
        pass_on(kind, 3, near, first, sibling)
        landed(kind, 1, near, second)
        pass_on(kind, 4, near, second, sibling)

    def complete(kind):
        others = 2 * parity + 1 - core, 2 * (1 - parity) + 1 - core
        total = pre_v[kind] + contract(kind, near)
        landed(kind, 2, others[0], whole)
        total += contract(kind, others[0])
        landed(kind, 3, others[1], first)
        landed(kind, 4, others[1], second)
        return total + contract(kind, others[1])

    summed = []
    def push(kind, lane, out, into, there):
        copy = pltpu.make_async_remote_copy(
            src_ref=out, dst_ref=into,
            send_sem=rs_send.at[kind, lane], recv_sem=rs_recv.at[kind, lane],
            device_id=(there, me), device_id_type=MESH,
        )
        copy.start()
        summed.append(copy)

    def partial_sums(kind, weights_of, units_of, distances):
        for d in distances:
            theirs = pl.ds(pl.multiple_of(shard(d, 1 - core) * feats, 32), feats)
            sib_out[kind, d] = nn(weights_of[theirs, :], units_of).astype(BF16)
            push(kind, d, sib_out.at[kind, d], sib_in.at[kind, d], sibling)
            ours = pl.ds(pl.multiple_of(shard(d, core) * feats, 32), feats)
            part[kind, d] = nn(weights_of[ours, :], units_of)

    def pair(kind, d):
        pltpu.make_async_copy(sib_in.at[kind, d], sib_in.at[kind, d], rs_recv.at[kind, d]).wait()
        return part[kind, d] + sib_in[kind, d].astype(F32)

    def came(kind, lane, into):
        pltpu.make_async_copy(into, into, rs_recv.at[kind, lane]).wait()
        return into[...].astype(F32)

    lower, higher = pl.ds(*halves[0]), pl.ds(*halves[1])

    def push_far(kind):
        total = pair(kind, 4).astype(BF16)
        right_out[kind, 0, lower] = total[:half]
        push(kind, 8, right_out.at[kind, 0, lower], right_in.at[kind, 0, lower], right_2)
        left_out[kind, 0, higher] = total[half:]
        push(kind, 12, left_out.at[kind, 0, higher], left_in.at[kind, 0, higher], left_2)
        right_out[kind, 1] = pair(kind, 3).astype(BF16)
        push(kind, 9, right_out.at[kind, 1], right_in.at[kind, 1], right)
        left_out[kind, 1] = pair(kind, 5).astype(BF16)
        push(kind, 13, left_out.at[kind, 1], left_in.at[kind, 1], left)

    def push_near(kind):
        right_out[kind, 2] = pair(kind, 1).astype(BF16)
        push(kind, 10, right_out.at[kind, 2], right_in.at[kind, 2], right)
        left_out[kind, 2] = pair(kind, 7).astype(BF16)
        push(kind, 14, left_out.at[kind, 2], left_in.at[kind, 2], left)
        part[kind, 2] = pair(kind, 2)
        part[kind, 6] = pair(kind, 6)
        part[kind, 0] = pair(kind, 0)

    def push_joined(kind):
        total = part[kind, 2] + came(kind, 9, right_in.at[kind, 1])
        right_out[kind, 3, higher] = total[half:].astype(BF16)
        right_out[kind, 3, lower] = (total[:half] + came(kind, 8, right_in.at[kind, 0, lower])).astype(BF16)
        push(kind, 11, right_out.at[kind, 3], right_in.at[kind, 3], right_2)
        total = part[kind, 6] + came(kind, 13, left_in.at[kind, 1])
        left_out[kind, 3, lower] = total[:half].astype(BF16)
        left_out[kind, 3, higher] = (total[half:] + came(kind, 12, left_in.at[kind, 0, higher])).astype(BF16)
        push(kind, 15, left_out.at[kind, 3], left_in.at[kind, 3], left_2)

    def summed_up(kind):
        total = part[kind, 0] + came(kind, 10, right_in.at[kind, 2]) + came(kind, 14, left_in.at[kind, 2])
        total += came(kind, 11, right_in.at[kind, 3]) + came(kind, 15, left_in.at[kind, 3])
        return total.astype(BF16)

    def weight_grads(group):
        grad_w_out[0, :, group * quarter : (group + 1) * quarter] = nt(preact_grad, gathered[0, group]).astype(BF16)

    arrive(0)
    arrive(1)
    relay(0)
    preact = complete(0)
    sigmoid_val = jax.nn.sigmoid(preact)
    hidden = (preact * sigmoid_val).astype(BF16)
    slope = sigmoid_val * (1.0 + preact * (1.0 - sigmoid_val))
    partial_sums(0, wout_r, hidden, (4, 3, 5))
    push_far(0)
    partial_sums(0, wout_r, hidden, (1, 7, 2, 6, 0))
    push_near(0)
    relay(1)
    preact_grad = (complete(1) * slope).astype(BF16)
    partial_sums(1, win_r, preact_grad, (4, 3, 5))
    push_joined(0)
    push_far(1)
    partial_sums(1, win_r, preact_grad, (1, 7, 2, 6, 0))
    push_near(1)
    weight_grads(0)
    weight_grads(1)
    push_joined(1)
    weight_grads(2)
    weight_grads(3)

    pieces = []
    for kind in range(2):
        total = summed_up(kind)
        pieces += [total[:LANES], jnp.concatenate([total[LANES:], jnp.zeros((LANES - upper, slots), BF16)], axis=0)]
    send2[...] = nt(perm[...], jnp.concatenate(pieces, axis=1)).astype(BF16).reshape(experts, 8, LANES)
    own2 = exchange(send2, recv2, 6)

    scaled_tok = [tok_s[:, i * LANES : (i + 1) * LANES].astype(F32) * gate_col[...] for i in range(2)]
    scaled_cot = [cot_s[:, i * LANES : (i + 1) * LANES].astype(F32) * gate_col[...] for i in range(2)]
    scale = 1.0 / member_v[:, :LANES]
    for copy in pending + summed:
        copy.wait_send()
    sent_all(send1.at[0], 0)
    sent_all(send1.at[1], 3)

    exchanged(own2, send2, recv2, 6)
    ordered = nn(perm_t[...], recv2[...].reshape(4 * slots, LANES))
    for i, (low, count) in enumerate(((0, LANES), (LANES, upper))):
        carried = ordered[i * slots : (i + 1) * slots] - centre_v[:, i * LANES : (i + 1) * LANES].astype(F32)
        pulled = (ordered[(2 + i) * slots : (3 + i) * slots] - back_v[:, i * LANES : (i + 1) * LANES]) * scale
        high, rest = split(carried)
        mixed = scaled_tok[i] + nn(weight_r[0], high) + nn(weight_r[0], rest) + nn(weight_r[1], high)
        mixed_out[:, low : low + count] = mixed[:, :count].astype(BF16)
        high, rest = split(pulled)
        grads = scaled_cot[i] + nn(either_r[...], high) + nn(either_r[...], rest)
        grad_tokens_out[:, low : low + count] = grads[:, :count].astype(BF16)
    sent_all(send2, 6)


def on_device(tokens, routes, gates, clusters, counts, w_in, w_out, cotangent):
    toks, width = tokens.shape
    experts = counts.shape[1]
    shards = lax.axis_size("dp")
    units = w_in.shape[2]
    feats = width // shards
    slots = experts * SLOTS
    vmem = pltpu.VMEM
    dma = pltpu.SemaphoreType.DMA
    scratch = [
        vmem((toks, 3 * LANES), BF16), vmem((toks, 3 * LANES), BF16),
        vmem((2, toks), jnp.int32), vmem((2, toks), F32), vmem((2, toks), jnp.int32), vmem((1, experts), jnp.int32),
        vmem((units, width), BF16), vmem((units, width), BF16),
        vmem((toks, width // 4), BF16), vmem((toks, width // 4), BF16),
        vmem((width, units), BF16), vmem((width, units), BF16),
        vmem((4 * slots, 4 * slots), BF16), vmem((4 * slots, 4 * slots), BF16),
        vmem((slots, toks), BF16), vmem((2, slots, toks), BF16),
        vmem((toks, slots), BF16), vmem((2, toks, slots), BF16),
        vmem((toks, LANES), F32), vmem((slots, 2 * LANES), F32),
        vmem((toks, 2 * LANES), BF16), vmem((toks, 2 * LANES), BF16),
        vmem((slots, 2 * LANES), BF16), vmem((slots, 2 * LANES), F32),
        vmem((2, experts, 8, 2 * LANES), BF16), vmem((2, experts, 8, 2 * LANES), BF16),
        vmem((experts, 8, LANES), BF16), vmem((experts, 8, LANES), BF16),
        vmem((2, 4, width // 4, slots), BF16), vmem((2, units, slots), F32),
        vmem((2, CHIPS, feats, slots), F32), vmem((2, CHIPS, feats, slots), BF16), vmem((2, CHIPS, feats, slots), BF16),
        vmem((2, 4, feats, slots), BF16), vmem((2, 4, feats, slots), BF16),
        vmem((2, 4, feats, slots), BF16), vmem((2, 4, feats, slots), BF16),
        dma((10,)), dma((9,)), dma((2, 5)), dma((2, 5)), dma((2, 16)), dma((2, 16)),
    ]
    operands = (tokens, routes.T, gates.T, clusters.T, counts, jnp.swapaxes(w_in, 1, 2), w_out, cotangent)
    operands = [pltpu.with_memory_space_constraint(operand, pltpu.HBM) for operand in operands]
    hbm = pl.BlockSpec(memory_space=pltpu.HBM)
    mixed, grad_tokens, grad_w = pl.pallas_call(
        functools.partial(kernel, (experts, toks, feats, units)),
        out_shape=(
            jax.ShapeDtypeStruct((toks, feats), BF16),
            jax.ShapeDtypeStruct((toks, feats), BF16),
            jax.ShapeDtypeStruct((1, units, width), BF16),
        ),
        in_specs=[hbm] * 8,
        out_specs=(pl.BlockSpec(memory_space=pltpu.VMEM),) * 3,
        scratch_shapes=scratch,
        compiler_params=pltpu.CompilerParams(
            collective_id=0, has_side_effects=True, vmem_limit_bytes=48 * 1024 * 1024
        ),
    )(*operands)
    return mixed, grad_tokens, jnp.swapaxes(grad_w, 1, 2)


def solution(mesh):
    in_specs = (
        P("expert", None),
        P("expert", None),
        P("expert", None),
        P("expert", None),
        P("expert", None),
        P("expert", None, "dp"),
        P("expert", "dp", None),
        P("expert", None),
    )
    out_specs = (P("expert", "dp"), P("expert", "dp"), P("expert", None, "dp"))
    return jax.shard_map(
        on_device, mesh=mesh, in_specs=in_specs, out_specs=out_specs, check_vma=False
    )
```

```python
import functools

import jax
import jax.numpy as jnp
from jax import lax
from jax.experimental import pallas as pl
from jax.experimental.pallas import tpu as pltpu
from jax.sharding import PartitionSpec as P

SLOTS = 2
LANES = 128
CHIPS = 8
MESH = pl.DeviceIdType.MESH
BF16 = jnp.bfloat16
F32 = jnp.float32

def nn(a, b):
    return lax.dot_general(a, b, (((1,), (0,)), ((), ())), preferred_element_type=F32)


def nt(a, b):
    return lax.dot_general(a, b, (((1,), (1,)), ((), ())), preferred_element_type=F32)


def split(value):
    high = value.astype(BF16)
    return high, (value - high.astype(F32)).astype(BF16)


def eye(size):
    rows = lax.broadcasted_iota(jnp.int32, (size, size), 0)
    return (rows == lax.broadcasted_iota(jnp.int32, (size, size), 1)).astype(BF16)


def kernel(
    shape,
    tokens, routes, gates, clusters, counts, w_in, w_out, cotangent,
    tokens_out, grad_w_out,
    tok_win, cot_win, routes_v, gates_v, clusters_v, counts_v, win_v, wout_v,
    tok_q, cot_q, win_r, wout_r, perm, perm_t,
    either_t, weight_t, either_r, weight_r, gate_col, member_v, tok_s, cot_s, centre_v, back_v,
    send1, recv1, send2, recv2,
    gathered, pre_v, part, sib_out, sib_in, right_out, left_out, right_in, left_in,
    in_sem, hop_sem, ag_send, ag_recv, rs_send, rs_recv,
):
    experts, toks, feats, units = shape
    slots = experts * SLOTS
    half = feats // 2
    halves = ((0, half), (half, half))
    upper = feats - LANES
    dp = lax.axis_index("dp")
    me = lax.axis_index("expert")
    chip = dp // 2
    core = lax.rem(dp, 2)
    right = lax.rem(chip + 1, CHIPS) * 2 + core
    left = lax.rem(chip + CHIPS - 1, CHIPS) * 2 + core
    right_2 = lax.rem(chip + 2, CHIPS) * 2 + core
    left_2 = lax.rem(chip + CHIPS - 2, CHIPS) * 2 + core
    sibling = chip * 2 + 1 - core

    def far_first(i):
        if experts != CHIPS * CHIPS:
            return lax.rem(me + i + 1, experts)

        def away(j):
            return 4 + (j + 1) // 2 * (1 - 2 * (j % 2))

        row = lax.rem(me // CHIPS + away(i // CHIPS), CHIPS)
        column = lax.rem(lax.rem(me, CHIPS) + away(i % CHIPS), CHIPS)
        return row * CHIPS + column

    def shard(distance, of_core):
        return lax.rem(chip + distance, CHIPS) * 2 + of_core

    width = tokens.shape[1]
    window = tok_win.shape[1]
    tile = jnp.minimum(dp * feats // LANES, (width - window) // LANES)
    start = pl.multiple_of(tile * LANES, LANES)
    shift = dp * feats - tile * LANES
    quarter = width // 4
    parity = lax.rem(chip, 2)
    mine, near = 2 * parity + core, 2 * (1 - parity) + core
    own_quarter = pl.ds(pl.multiple_of(mine * quarter, LANES), quarter)

    loads = [
        pltpu.make_async_copy(src, dst, in_sem.at[i])
        for i, (src, dst) in enumerate((
            (routes, routes_v), (clusters, clusters_v), (gates, gates_v), (counts, counts_v),
            (tokens.at[:, own_quarter], tok_q),
            (cotangent.at[:, own_quarter], cot_q),
            (tokens.at[:, pl.ds(start, window)], tok_win),
            (cotangent.at[:, pl.ds(start, window)], cot_win),
            (w_out.at[0], wout_v), (w_in.at[0], win_v),
        ))
    ]
    for load in loads[:6]:
        load.start()

    barrier = pltpu.get_barrier_semaphore()

    @pl.loop(0, experts - 1)
    def _(i):
        pl.semaphore_signal(barrier, inc=1, device_id=(dp, far_first(i)), device_id_type=MESH)

    for there in (right, left, right_2, left_2, sibling):
        pl.semaphore_signal(barrier, inc=1, device_id=(there, me), device_id_type=MESH)

    for load in loads[6:]:
        load.start()

    rows = lax.broadcasted_iota(jnp.int32, (4 * slots, 4 * slots), 0)
    cols = lax.broadcasted_iota(jnp.int32, (4 * slots, 4 * slots), 1)
    perm[...] = (cols == ((rows % 8) // 2) * slots + (rows // 8) * 2 + rows % 2).astype(F32).astype(BF16)

    for load in loads[:4]:
        load.wait()
    expert_rows = lax.broadcasted_iota(jnp.int32, (experts, experts), 0)
    expert_cols = lax.broadcasted_iota(jnp.int32, (experts, experts), 1)
    live_col = jnp.sum(jnp.where(expert_rows == expert_cols, counts_v[...], 0), axis=1, keepdims=True)
    ids = lax.broadcasted_iota(jnp.int32, (experts, toks), 0)
    slot_rows = lax.broadcasted_iota(jnp.int32, (slots, toks), 0)
    hits, weights = [], []
    for k in range(2):
        route = routes_v[k : k + 1, :]
        live = jnp.sum(jnp.where(ids == route, live_col, 0), axis=0, keepdims=True)
        slot = route * SLOTS + jnp.where(live == 2, clusters_v[k : k + 1, :] & 1, 0)
        hits.append((slot_rows == slot).astype(F32))
        weights.append(hits[-1] * gates_v[k : k + 1, :])
    either = hits[0] + hits[1]
    weight_hi, weight_lo = split(weights[0] + weights[1])
    member = jnp.maximum(jnp.sum(either, axis=1, keepdims=True), 1.0)
    member_v[...] = jnp.broadcast_to(member, member_v.shape)
    either_t[...] = either.astype(BF16)
    weight_t[0] = weight_hi
    weight_t[1] = weight_lo

    def exchange(send, recv, sem):
        own = pltpu.make_async_copy(send.at[me], recv.at[me], hop_sem.at[sem])
        own.start()

        @pl.loop(0, experts - 1)
        def _(i):
            peer = far_first(i)
            pltpu.make_async_remote_copy(
                src_ref=send.at[peer], dst_ref=recv.at[me],
                send_sem=hop_sem.at[sem + 1], recv_sem=hop_sem.at[sem + 2],
                device_id=(dp, peer), device_id_type=MESH,
            ).start()

        return own

    def exchanged(own, send, recv, sem):
        own.wait()
        rest = pl.ds(0, experts - 1)
        pltpu.make_async_copy(recv.at[rest], recv.at[rest], hop_sem.at[sem + 2]).wait()

    def sent_all(send, sem):
        rest = pl.ds(0, experts - 1)
        pltpu.make_async_copy(send.at[rest], send.at[rest], hop_sem.at[sem + 1]).wait()

    def spread(rows_of):
        last = jnp.concatenate([rows_of[:, 6 * LANES :], jnp.zeros((slots, LANES), BF16)], axis=1)
        stacked = jnp.concatenate([rows_of[:, 2 * i * LANES : 2 * (i + 1) * LANES] for i in range(3)] + [last], axis=0)
        return nn(perm[...], stacked).astype(BF16).reshape(experts, 8, 2 * LANES)

    loads[4].wait()
    send1[0] = spread((nn(either_t[...], tok_q[...]) / member).astype(BF16))
    pl.semaphore_wait(barrier, experts + 4)
    owns = [exchange(send1.at[0], recv1.at[0], 0)]
    loads[5].wait()
    send1[1] = spread((nn(weight_t[0], cot_q[...]) + nn(weight_t[1], cot_q[...])).astype(BF16))
    owns.append(exchange(send1.at[1], recv1.at[1], 3))

    pick_rows = lax.broadcasted_iota(jnp.int32, (window, 2 * LANES), 0)
    pick_cols = lax.broadcasted_iota(jnp.int32, (window, 2 * LANES), 1)
    pick = ((pick_rows == pick_cols + shift) & (pick_cols < feats)).astype(F32).astype(BF16)
    loads[6].wait()
    tok_s[...] = nn(tok_win[...], pick).astype(BF16)
    centre_v[...] = (nn(either_t[...], tok_s[...]) / member_v[...]).astype(BF16)
    loads[7].wait()
    cot_s[...] = nn(cot_win[...], pick).astype(BF16)
    back_v[...] = nn(weight_t[0], cot_s[...]) + nn(weight_t[1], cot_s[...])
    perm_t[...] = (rows == ((cols % 8) // 2) * slots + (cols // 8) * 2 + cols % 2).astype(F32).astype(BF16)
    token_eye = eye(toks)
    either_r[...] = nt(token_eye, either_t[...]).astype(BF16)
    weight_r[0] = nt(token_eye, weight_t[0]).astype(BF16)
    weight_r[1] = nt(token_eye, weight_t[1]).astype(BF16)
    gate_row = 1.0 + jnp.sum(gates_v[...], axis=0, keepdims=True)
    gate_col[...] = jnp.broadcast_to(
        jnp.sum(jnp.where(token_eye.astype(F32) > 0.0, gate_row, 0.0), axis=1, keepdims=True), gate_col.shape
    )
    loads[8].wait()
    loads[9].wait()
    lane_eye = eye(2 * LANES)

    @pl.loop(0, width // (2 * LANES))
    def _(j):
        at = pl.ds(pl.multiple_of(j * 2 * LANES, LANES), 2 * LANES)
        win_r[at, :] = nt(lane_eye, win_v[:, at]).astype(BF16)
        wout_r[at, :] = nt(lane_eye, wout_v[:, at]).astype(BF16)

    pending = []

    def pass_on(kind, lane, which, rows, there):
        at = pl.ds(*rows)
        copy = pltpu.make_async_remote_copy(
            src_ref=gathered.at[kind, which, at], dst_ref=gathered.at[kind, which, at],
            send_sem=ag_send.at[kind, lane], recv_sem=ag_recv.at[kind, lane],
            device_id=(there, me), device_id_type=MESH,
        )
        copy.start()
        pending.append(copy)

    def landed(kind, lane, which, rows):
        here = gathered.at[kind, which, pl.ds(*rows)]
        pltpu.make_async_copy(here, here, ag_recv.at[kind, lane]).wait()

    whole, first, second = (0, quarter), (0, quarter // 2), (quarter // 2, quarter // 2)
    projections = (win_v, wout_v)

    def contract(kind, which):
        columns = pl.ds(pl.multiple_of(which * quarter, LANES), quarter)
        return nn(projections[kind][:, columns], gathered[kind, which])

    def arrive(kind):
        exchanged(owns[kind], send1.at[kind], recv1.at[kind], 3 * kind)
        arrived = lax.dot_general(
            recv1[kind].reshape(4 * slots, 2 * LANES), perm[...], (((0,), (0,)), ((), ())), preferred_element_type=F32
        ).astype(BF16)
        for i in range(4):
            count = 2 * LANES if i < 3 else LANES
            low = 2 * i * LANES
            gathered[kind, mine, low : low + count, :] = arrived[:count, i * slots : (i + 1) * slots]
        pass_on(kind, 0, mine, first, right)
        pass_on(kind, 1, mine, second, left)
        pass_on(kind, 2, mine, whole, sibling)
        pre_v[kind] = contract(kind, mine)

    def relay(kind):
        landed(kind, 0, near, first)
        pass_on(kind, 3, near, first, sibling)
        landed(kind, 1, near, second)
        pass_on(kind, 4, near, second, sibling)

    def complete(kind):
        others = 2 * parity + 1 - core, 2 * (1 - parity) + 1 - core
        total = pre_v[kind] + contract(kind, near)
        landed(kind, 2, others[0], whole)
        total += contract(kind, others[0])
        landed(kind, 3, others[1], first)
        landed(kind, 4, others[1], second)
        return total + contract(kind, others[1])

    summed = []
    def push(kind, lane, out, into, there):
        copy = pltpu.make_async_remote_copy(
            src_ref=out, dst_ref=into,
            send_sem=rs_send.at[kind, lane], recv_sem=rs_recv.at[kind, lane],
            device_id=(there, me), device_id_type=MESH,
        )
        copy.start()
        summed.append(copy)

    def partial_sums(kind, weights_of, units_of, distances):
        for d in distances:
            theirs = pl.ds(pl.multiple_of(shard(d, 1 - core) * feats, 32), feats)
            sib_out[kind, d] = nn(weights_of[theirs, :], units_of).astype(BF16)
            push(kind, d, sib_out.at[kind, d], sib_in.at[kind, d], sibling)
            ours = pl.ds(pl.multiple_of(shard(d, core) * feats, 32), feats)
            part[kind, d] = nn(weights_of[ours, :], units_of)

    def pair(kind, d):
        pltpu.make_async_copy(sib_in.at[kind, d], sib_in.at[kind, d], rs_recv.at[kind, d]).wait()
        return part[kind, d] + sib_in[kind, d].astype(F32)

    def came(kind, lane, into):
        pltpu.make_async_copy(into, into, rs_recv.at[kind, lane]).wait()
        return into[...].astype(F32)

    lower, higher = pl.ds(*halves[0]), pl.ds(*halves[1])

    def push_far(kind):
        total = pair(kind, 4).astype(BF16)
        right_out[kind, 0, lower] = total[:half]
        push(kind, 8, right_out.at[kind, 0, lower], right_in.at[kind, 0, lower], right_2)
        left_out[kind, 0, higher] = total[half:]
        push(kind, 12, left_out.at[kind, 0, higher], left_in.at[kind, 0, higher], left_2)
        right_out[kind, 1] = pair(kind, 3).astype(BF16)
        push(kind, 9, right_out.at[kind, 1], right_in.at[kind, 1], right)
        left_out[kind, 1] = pair(kind, 5).astype(BF16)
        push(kind, 13, left_out.at[kind, 1], left_in.at[kind, 1], left)

    def push_near(kind):
        right_out[kind, 2] = pair(kind, 1).astype(BF16)
        push(kind, 10, right_out.at[kind, 2], right_in.at[kind, 2], right)
        left_out[kind, 2] = pair(kind, 7).astype(BF16)
        push(kind, 14, left_out.at[kind, 2], left_in.at[kind, 2], left)
        part[kind, 2] = pair(kind, 2)
        part[kind, 6] = pair(kind, 6)
        part[kind, 0] = pair(kind, 0)

    def push_joined(kind):
        total = part[kind, 2] + came(kind, 9, right_in.at[kind, 1])
        right_out[kind, 3, higher] = total[half:].astype(BF16)
        right_out[kind, 3, lower] = (total[:half] + came(kind, 8, right_in.at[kind, 0, lower])).astype(BF16)
        push(kind, 11, right_out.at[kind, 3], right_in.at[kind, 3], right_2)
        total = part[kind, 6] + came(kind, 13, left_in.at[kind, 1])
        left_out[kind, 3, lower] = total[:half].astype(BF16)
        left_out[kind, 3, higher] = (total[half:] + came(kind, 12, left_in.at[kind, 0, higher])).astype(BF16)
        push(kind, 15, left_out.at[kind, 3], left_in.at[kind, 3], left_2)

    def summed_up(kind):
        total = part[kind, 0] + came(kind, 10, right_in.at[kind, 2]) + came(kind, 14, left_in.at[kind, 2])
        total += came(kind, 11, right_in.at[kind, 3]) + came(kind, 15, left_in.at[kind, 3])
        return total.astype(BF16)

    def weight_grads(group):
        grad_w_out[0, :, group * quarter : (group + 1) * quarter] = nt(preact_grad, gathered[0, group]).astype(BF16)

    arrive(0)
    arrive(1)
    relay(0)
    preact = complete(0)
    sigmoid_val = jax.nn.sigmoid(preact)
    hidden = (preact * sigmoid_val).astype(BF16)
    slope = sigmoid_val * (1.0 + preact * (1.0 - sigmoid_val))
    partial_sums(0, wout_r, hidden, (4, 3, 5))
    push_far(0)
    partial_sums(0, wout_r, hidden, (1, 7, 2, 6, 0))
    push_near(0)
    relay(1)
    preact_grad = (complete(1) * slope).astype(BF16)
    partial_sums(1, win_r, preact_grad, (4, 3, 5))
    push_joined(0)
    push_far(1)
    partial_sums(1, win_r, preact_grad, (1, 7, 2, 6, 0))
    push_near(1)
    weight_grads(0)
    weight_grads(1)
    push_joined(1)
    weight_grads(2)
    weight_grads(3)

    pieces = []
    for kind in range(2):
        total = summed_up(kind)
        pieces += [total[:LANES], jnp.concatenate([total[LANES:], jnp.zeros((LANES - upper, slots), BF16)], axis=0)]
    send2[...] = nt(perm[...], jnp.concatenate(pieces, axis=1)).astype(BF16).reshape(experts, 8, LANES)
    own2 = exchange(send2, recv2, 6)

    scaled_tok = [tok_s[:, i * LANES : (i + 1) * LANES].astype(F32) * gate_col[...] for i in range(2)]
    scaled_cot = [cot_s[:, i * LANES : (i + 1) * LANES].astype(F32) * gate_col[...] for i in range(2)]
    scale = 1.0 / member_v[:, :LANES]
    for copy in pending + summed:
        copy.wait_send()
    sent_all(send1.at[0], 0)
    sent_all(send1.at[1], 3)

    exchanged(own2, send2, recv2, 6)
    ordered = nn(perm_t[...], recv2[...].reshape(4 * slots, LANES))
    for i, (low, count) in enumerate(((0, LANES), (LANES, upper))):
        carried = ordered[i * slots : (i + 1) * slots] - centre_v[:, i * LANES : (i + 1) * LANES].astype(F32)
        pulled = (ordered[(2 + i) * slots : (3 + i) * slots] - back_v[:, i * LANES : (i + 1) * LANES]) * scale
        high, rest = split(carried)
        mixed = scaled_tok[i] + nn(weight_r[0], high) + nn(weight_r[0], rest) + nn(weight_r[1], high)
        tokens_out[0, :, low : low + count] = mixed[:, :count].astype(BF16)
        high, rest = split(pulled)
        grads = scaled_cot[i] + nn(either_r[...], high) + nn(either_r[...], rest)
        tokens_out[1, :, low : low + count] = grads[:, :count].astype(BF16)
    sent_all(send2, 6)


def on_device(tokens, routes, gates, clusters, counts, w_in, w_out, cotangent):
    toks, width = tokens.shape
    experts = counts.shape[1]
    shards = lax.axis_size("dp")
    units = w_in.shape[2]
    feats = width // shards
    slots = experts * SLOTS
    vmem = pltpu.VMEM
    dma = pltpu.SemaphoreType.DMA
    scratch = [
        vmem((toks, 3 * LANES), BF16), vmem((toks, 3 * LANES), BF16),
        vmem((2, toks), jnp.int32), vmem((2, toks), F32), vmem((2, toks), jnp.int32), vmem((1, experts), jnp.int32),
        vmem((units, width), BF16), vmem((units, width), BF16),
        vmem((toks, width // 4), BF16), vmem((toks, width // 4), BF16),
        vmem((width, units), BF16), vmem((width, units), BF16),
        vmem((4 * slots, 4 * slots), BF16), vmem((4 * slots, 4 * slots), BF16),
        vmem((slots, toks), BF16), vmem((2, slots, toks), BF16),
        vmem((toks, slots), BF16), vmem((2, toks, slots), BF16),
        vmem((toks, LANES), F32), vmem((slots, 2 * LANES), F32),
        vmem((toks, 2 * LANES), BF16), vmem((toks, 2 * LANES), BF16),
        vmem((slots, 2 * LANES), BF16), vmem((slots, 2 * LANES), F32),
        vmem((2, experts, 8, 2 * LANES), BF16), vmem((2, experts, 8, 2 * LANES), BF16),
        vmem((experts, 8, LANES), BF16), vmem((experts, 8, LANES), BF16),
        vmem((2, 4, width // 4, slots), BF16), vmem((2, units, slots), F32),
        vmem((2, CHIPS, feats, slots), F32), vmem((2, CHIPS, feats, slots), BF16), vmem((2, CHIPS, feats, slots), BF16),
        vmem((2, 4, feats, slots), BF16), vmem((2, 4, feats, slots), BF16),
        vmem((2, 4, feats, slots), BF16), vmem((2, 4, feats, slots), BF16),
        dma((10,)), dma((9,)), dma((2, 5)), dma((2, 5)), dma((2, 16)), dma((2, 16)),
    ]
    operands = (tokens, routes.T, gates.T, clusters.T, counts, jnp.swapaxes(w_in, 1, 2), w_out, cotangent)
    operands = [pltpu.with_memory_space_constraint(operand, pltpu.HBM) for operand in operands]
    hbm = pl.BlockSpec(memory_space=pltpu.HBM)
    token_results, grad_w = pl.pallas_call(
        functools.partial(kernel, (experts, toks, feats, units)),
        out_shape=(
            jax.ShapeDtypeStruct((2, toks, feats), BF16),
            jax.ShapeDtypeStruct((1, units, width), BF16),
        ),
        in_specs=[hbm] * 8,
        out_specs=(pl.BlockSpec(memory_space=pltpu.VMEM),) * 2,
        scratch_shapes=scratch,
        compiler_params=pltpu.CompilerParams(
            collective_id=0, has_side_effects=True, vmem_limit_bytes=48 * 1024 * 1024
        ),
    )(*operands)
    return token_results[0], token_results[1], jnp.swapaxes(grad_w, 1, 2)


def solution(mesh):
    in_specs = (
        P("expert", None),
        P("expert", None),
        P("expert", None),
        P("expert", None),
        P("expert", None),
        P("expert", None, "dp"),
        P("expert", "dp", None),
        P("expert", None),
    )
    out_specs = (P("expert", "dp"), P("expert", "dp"), P("expert", None, "dp"))
    return jax.shard_map(
        on_device, mesh=mesh, in_specs=in_specs, out_specs=out_specs, check_vma=False
    )
```
